32 devices in a mesh: shard: 8 (over z, core), replica: 4 (over y, x).
Axes of the slice: x: 2, y: 2, z: 4, core: 2. Of those that a mesh axis runs over, the one named last changes fastest.
Arguments:
- activations: bfloat16 [2, 2048, 8192], P(None, ('shard', 'replica')), may hold values from -6 to 6
- residual: bfloat16 [2, 2048, 4096], P(None, ('shard', 'replica')), may hold values from -6 to 6
- down_weight: bfloat16 [8192, 4096], P('shard'), may hold values from -0.0625 to 0.0625
- norm_gain: float32 [4096], replicated, may hold values from 0.5 to 1.5
- hard_owner: int32 [2048, 7], P(('shard', 'replica')), may hold values from 0 to 31, all different within a row; in each aligned block of 64 rows (0 to 63, 64 to 127, ...) at most 15 rows name the same one
- hard_row: int32 [2048, 7], P(('shard', 'replica')), may hold values from 0 to 63
Outputs:
- mean_loss: float32 [], replicated
- weight_grad: float32 [8192, 4096], P('shard')
- gain_grad: float32 [4096], replicated
The draws below stay inside these ranges and needn't reach their ends.
Inputs may be any that keep to these rules, and one draw needn't show every extreme that they name: `hard_owner`: the 7 owners of one query are distinct. Among the 64 queries of one device no device is named more than 15 times, and this bound is met on some devices.
All inputs are finite; a program needn't handle non-finite values.
Results may differ from the reference program's by a relative error of at most 0.025.
Values may be sent and summed in bfloat16 or wider, within the bound.
A program may use at most 128 MiB of HBM per device.

```python
import math
import jax
import jax.numpy as jnp
import numpy as np
from jax import lax

HIDDEN_SIZE_DIM = 4096
FFW = 8192
Q_DEV = 64
HARD = 7
SAMPLE_NUMBER = 2048
CAP = 15
N_SHARD = 8
N_REPLICA = 4
DEVICES = 32


def set_ends(values, rng, least, high):
    dims = values.shape
    spot = [jax.random.randint(jax.random.fold_in(rng, axis), (), 0, dims[axis]) for axis in range(len(dims))]
    values = values.at[tuple(spot)].set(least)
    longest = dims.index(max(dims))
    spot[longest] = (spot[longest] + 1) % dims[longest]
    return values.at[tuple(spot)].set(high)


def block_scale(rng, dims, pieces, least, top_value):
    def one(axis_at, shards_of):
        steps = jax.random.uniform(jax.random.fold_in(jax.random.fold_in(rng, 6), axis_at), (shards_of,), jnp.float32, least / len(pieces), top_value / len(pieces))
        return jnp.repeat(jnp.exp(steps), dims[axis_at] // shards_of).reshape((-1,) + (1,) * (len(dims) - axis_at - 1))

    level = one(*pieces[0])
    for cut in pieces[1:]:
        level = level * one(*cut)
    return level


def routed_block(rng, own, number, rows, count, top, bound, slope):
    ranking = jax.random.permutation(rng, count)
    heavy_load, usual = shares(count, rows * top, bound, slope, True), shares(count, rows * top, bound, slope, False)
    places = jnp.arange(count)

    def named(tallies, offset_by):
        used = int((tallies > 0).sum())
        fixed = max(1, used // 4)
        moved = fixed + (places - fixed + offset_by * (used - fixed)) % max(1, count - fixed)
        return jnp.zeros((count,), jnp.int32).at[ranking[jnp.where(places < fixed, places, moved)]].set(jnp.asarray(tallies, jnp.int32))

    tallies = jnp.where(number % 4 == 0, named(heavy_load, number // 4), named(usual, number - number // 4 - 1))
    mixed = jax.random.permutation(jax.random.fold_in(own, 3), count)
    donor, taker = mixed[0:count // 2 * 2:2], mixed[1:count // 2 * 2:2]
    slack = jnp.minimum(tallies[donor] - 1, bound - tallies[taker]) // 2
    slack = jnp.where((donor == ranking[0]) | (taker == ranking[0]) | (tallies[taker] == 0), 0, jnp.maximum(slack, 0))
    moved = jax.random.randint(jax.random.fold_in(own, 4), (count // 2,), 0, 1 << 20) % (slack + 1)
    tallies = tallies.at[donor].add(-moved).at[taker].add(moved)
    labels = jnp.searchsorted(jnp.cumsum(tallies), jnp.arange(rows * top), side="right").astype(jnp.int32)
    grid = labels.reshape(top, rows).T
    grid = grid[jax.random.permutation(jax.random.fold_in(own, 1), rows)]
    offset_by = jax.random.randint(jax.random.fold_in(own, 2), (rows, 1), 0, top)
    return jnp.take_along_axis(grid, (jnp.arange(top)[None, :] + offset_by) % top, axis=1)


def shares(number_of, total, most, slope, full):
    portions = [(1 << 20) // math.isqrt(grade ** slope) + 1 for grade in range(1, number_of + 1)]
    largest = most if full else min(most, max(-(-total // number_of), total * portions[0] // sum(portions)))
    least = 1 if total - largest >= number_of - 1 else 0
    counts, rest = [largest] + [least] * (number_of - 1), total - largest - least * (number_of - 1)
    while rest > 0:
        free = [i for i in range(1, number_of) if counts[i] < largest] or [i for i in range(1, number_of) if counts[i] < most]
        pool, budget = sum([portions[i] for i in free]), rest
        for i in free:
            extra = min(most - counts[i], max(1, budget * portions[i] // pool), rest)
            counts[i] = counts[i] + extra
            rest = rest - extra
    return np.array(counts)


def gaussian(stream_key, shape, scale, limit, shards=(), held_as=jnp.bfloat16):
    factor_of = block_scale(stream_key, shape, shards, -0.22, 0.18) if shards else 1.0
    drawn = jax.random.normal(stream_key, shape, jnp.float32) * scale * factor_of
    return jnp.minimum(jnp.maximum(drawn, -limit), limit).astype(held_as)


def setup_inputs(seed: int = 0) -> dict:
    keys = jax.random.split(jax.random.key(seed), 7)
    activations = gaussian(keys[0], (2, SAMPLE_NUMBER, FFW), 1.0, 6.0, ((1, 32),))
    residual = gaussian(keys[1], (2, SAMPLE_NUMBER, HIDDEN_SIZE_DIM), 1.0, 6.0, ((1, 32),))
    down_weight = gaussian(keys[2], (FFW, HIDDEN_SIZE_DIM), FFW ** -0.5, 0.0625, ((0, 8),))
    norm_gain = jnp.clip(1.0 + 0.1 * jax.random.normal(keys[3], (HIDDEN_SIZE_DIM,), jnp.float32), 0.5, 1.5)
    hard_owner_keys = jax.random.split(jax.random.fold_in(keys[4], 1), SAMPLE_NUMBER // Q_DEV)
    hard_owner_turns = jax.random.permutation(jax.random.fold_in(keys[4], 3), SAMPLE_NUMBER // Q_DEV)
    hard_owner = jax.vmap(lambda own, number: routed_block(jax.random.fold_in(keys[4], 2), own, number, Q_DEV, DEVICES, HARD, CAP, 2))(hard_owner_keys, hard_owner_turns).reshape((SAMPLE_NUMBER, HARD))
    hard_row = set_ends(jax.random.randint(keys[5], (SAMPLE_NUMBER, HARD), 0, Q_DEV), jax.random.fold_in(keys[5], 1), 0, Q_DEV - 1).astype(jnp.int32)
    return dict(activations=activations, residual=residual, down_weight=down_weight, norm_gain=norm_gain, hard_owner=hard_owner, hard_row=hard_row)


epsilon = 1e-05
sharpness_divisor = 0.02

def normalize_rows(stream, norm_gain):
    inv_rms = lax.rsqrt(lax.optimization_barrier(jnp.mean(stream * stream, axis=-1, keepdims=True)) + epsilon)
    normed = stream * inv_rms
    scaled = normed * norm_gain
    length = jnp.sqrt(lax.optimization_barrier(jnp.sum(scaled * scaled, axis=-1, keepdims=True)))
    return (inv_rms, normed, length, scaled / length)

def backward_rows(normalized_entry_sensitivity, inv_rms, normed, length, unit_f32, norm_gain):
    grad_scaled = (normalized_entry_sensitivity - unit_f32 * lax.optimization_barrier(jnp.sum(unit_f32 * normalized_entry_sensitivity, axis=-1, keepdims=True))) / length
    gain_terms = lax.optimization_barrier(jnp.sum(grad_scaled * normed, axis=0))
    grad_normed = grad_scaled * norm_gain
    grad_stream = inv_rms * (grad_normed - normed * lax.optimization_barrier(jnp.mean(grad_normed * normed, axis=-1, keepdims=True)))
    return (gain_terms, grad_stream.astype(jnp.bfloat16))

def softmax_terms(shared_pool_affinity, mined_distractor_affinity):
    width = shared_pool_affinity.shape[-1]
    cosine_affinity_matrix = jnp.concatenate([shared_pool_affinity, mined_distractor_affinity], axis=-1) / sharpness_divisor
    expo = jnp.exp(cosine_affinity_matrix)
    totals = lax.optimization_barrier(jnp.sum(expo, axis=-1, keepdims=True))
    matching_target_index = jnp.diagonal(shared_pool_affinity, axis1=-2, axis2=-1) / sharpness_divisor
    losses = jnp.log(totals[..., 0]) - matching_target_index
    identity = jnp.broadcast_to(jnp.eye(width, dtype=jnp.float32), shared_pool_affinity.shape)
    target = jnp.concatenate([identity, jnp.zeros_like(mined_distractor_affinity)], axis=-1)
    weights = (expo / totals - target).astype(jnp.bfloat16)
    return (jnp.sum(losses), weights[..., :width], weights[..., width:])

def reference(activations, residual, down_weight, norm_gain, hard_owner, hard_row):
    devices = N_SHARD * N_REPLICA
    flat_act = activations.reshape(-1, FFW)
    block = FFW // N_SHARD
    mixed = jnp.zeros((flat_act.shape[0], HIDDEN_SIZE_DIM), jnp.float32)
    for shard_index in range(N_SHARD):
        term = jnp.dot(flat_act[:, shard_index * block:(shard_index + 1) * block], down_weight[shard_index * block:(shard_index + 1) * block], preferred_element_type=jnp.float32)
        rounded = lax.optimization_barrier(term.astype(jnp.bfloat16))
        mixed = mixed + rounded.astype(jnp.float32)
    stream = residual.reshape(-1, HIDDEN_SIZE_DIM).astype(jnp.float32) + mixed
    inv_rms, normed, length, unit_f32 = normalize_rows(stream, norm_gain)
    unit = unit_f32.astype(jnp.bfloat16)
    flat_query = unit[:SAMPLE_NUMBER]
    flat_pass = unit[SAMPLE_NUMBER:]
    passage_id = (hard_owner * Q_DEV + hard_row).astype(jnp.int32)

    def per_device(items):
        query, passage, ident = items
        hard = flat_pass[ident]
        local = jnp.dot(query, passage.T, preferred_element_type=jnp.float32)
        mined_distractor_affinity = jnp.einsum('qd,qkd->qk', query.astype(jnp.float32), hard.astype(jnp.float32))
        loss_sum, grad_local, grad_hard = softmax_terms(local, mined_distractor_affinity)
        request_sensitivity = jnp.dot(grad_local, passage, preferred_element_type=jnp.float32)
        request_sensitivity = request_sensitivity + jnp.einsum('qk,qkd->qd', grad_hard.astype(jnp.float32), hard.astype(jnp.float32))
        document_sensitivity = jnp.dot(grad_local.T, query, preferred_element_type=jnp.float32)
        return (loss_sum, grad_hard, request_sensitivity, document_sensitivity)
    losses, grad_hard, request_sensitivity, document_sensitivity = lax.map(per_device, (flat_query.reshape(devices, Q_DEV, HIDDEN_SIZE_DIM), flat_pass.reshape(devices, Q_DEV, HIDDEN_SIZE_DIM), passage_id.reshape(devices, Q_DEV, HARD)))
    grad_hard = grad_hard.reshape(SAMPLE_NUMBER, HARD).astype(jnp.float32)
    document_sensitivity = document_sensitivity.reshape(SAMPLE_NUMBER, HIDDEN_SIZE_DIM)
    query_f32 = flat_query.astype(jnp.float32)
    for slot in range(HARD):
        document_sensitivity = document_sensitivity.at[passage_id[:, slot]].add(grad_hard[:, slot, None] * query_f32)
    normalized_entry_sensitivity = jnp.concatenate([request_sensitivity.reshape(SAMPLE_NUMBER, HIDDEN_SIZE_DIM), document_sensitivity], axis=0) / sharpness_divisor
    gain_grad, grad_stream = backward_rows(normalized_entry_sensitivity, inv_rms, normed, length, unit_f32, norm_gain)
    weight_grad = jnp.dot(flat_act.T, grad_stream, preferred_element_type=jnp.float32)
    mean_loss = jnp.sum(losses) / SAMPLE_NUMBER
    return (mean_loss, weight_grad, gain_grad)
```

```python
import functools

import jax
import jax.numpy as jnp
from jax import lax
from jax.experimental import pallas as pl
from jax.experimental.pallas import tpu as pltpu
from jax.sharding import PartitionSpec as P

HARD = 7
LANES = 128


epsilon = 1e-05
sharpness_divisor = 0.02


def normalize_rows(stream, norm_gain):
    inv_rms = lax.rsqrt(jnp.mean(stream * stream, axis=-1, keepdims=True) + epsilon)
    normed = stream * inv_rms
    scaled = normed * norm_gain
    length = jnp.sqrt(jnp.sum(scaled * scaled, axis=-1, keepdims=True))
    return (inv_rms, length, scaled / length)


def softmax_terms(local_score, hard_score):
    width = local_score.shape[-1]
    logits = jnp.concatenate([local_score, hard_score], axis=-1) / sharpness_divisor
    expo = jnp.exp(logits)
    totals = jnp.sum(expo, axis=-1, keepdims=True)
    positive = jnp.diagonal(local_score) / sharpness_divisor
    losses = jnp.log(totals[:, 0]) - positive
    identity = jnp.eye(width, dtype=jnp.float32)
    target = jnp.concatenate([identity, jnp.zeros_like(hard_score)], axis=-1)
    weights = (expo / totals - target).astype(jnp.bfloat16).astype(jnp.float32)
    return (losses[:, None], weights, weights * logits)


def pick_kernel(q_ref, p_ref, name_ref, out_ref):
    score = lax.dot_general(
        q_ref[...], p_ref[...], (((1,), (1,)), ((), ())), preferred_element_type=jnp.float32
    )
    name = name_ref[...]
    lane, group = name % LANES, name // LANES
    found = jnp.zeros(out_ref.shape, jnp.float32)
    for block in range(p_ref.shape[0] // LANES):
        here = jnp.take_along_axis(score[:, block * LANES : (block + 1) * LANES], lane, axis=1)
        found = jnp.where(group == block, here, found)
    out_ref[...] = found


def pick_scores(queries, passages, names, block):
    total, feats = queries.shape
    return pl.pallas_call(
        pick_kernel,
        grid=(total // block,),
        in_specs=[
            pl.BlockSpec((block, feats), lambda i: (i, 0)),
            pl.BlockSpec((total, feats), lambda i: (0, 0)),
            pl.BlockSpec((block, LANES), lambda i: (i, 0)),
        ],
        out_specs=pl.BlockSpec((block, LANES), lambda i: (i, 0)),
        out_shape=jax.ShapeDtypeStruct((total, LANES), jnp.float32),
        compiler_params=pltpu.CompilerParams(vmem_limit_bytes=48 * 1024 * 1024),
    )(queries, passages, names)


def spread_kernel(group_rows, q_ref, p_ref, name_ref, pack_ref, gq_ref, gp_ref, tp_ref):
    step = pl.program_id(0)

    @pl.when(step == 0)
    def _():
        gp_ref[...] = jnp.zeros_like(gp_ref)
        tp_ref[...] = jnp.zeros_like(tp_ref)

    block, total = q_ref.shape[0], p_ref.shape[0]
    column = lax.broadcasted_iota(jnp.int32, (block, total), 1)
    weight = jnp.zeros((block, total), jnp.float32)
    share = jnp.zeros((block, total), jnp.float32)
    for k in range(HARD):
        hit = column == name_ref[:, k : k + 1]
        weight = jnp.where(hit, pack_ref[:, group_rows + k : group_rows + k + 1], weight)
        share = jnp.where(
            hit, pack_ref[:, group_rows + HARD + k : group_rows + HARD + k + 1], share
        )
    tp_ref[...] += jnp.sum(share, axis=0, keepdims=True)
    weight = weight.astype(jnp.bfloat16)
    gq_ref[...] = jnp.dot(weight, p_ref[...], preferred_element_type=jnp.float32)
    gp_ref[...] += lax.dot_general(
        weight, q_ref[...], (((0,), (0,)), ((), ())), preferred_element_type=jnp.float32
    )
    for part in range(block // group_rows):
        mine = slice(part * group_rows, (part + 1) * group_rows)
        there = pl.ds(pl.multiple_of(step * block + part * group_rows, group_rows), group_rows)
        local = pack_ref[mine, :group_rows].astype(jnp.bfloat16)
        gq_ref[mine, :] += jnp.dot(local, p_ref[there, :], preferred_element_type=jnp.float32)
        gp_ref[there, :] += lax.dot_general(
            local, q_ref[mine, :], (((0,), (0,)), ((), ())), preferred_element_type=jnp.float32
        )


def spread_grads(queries, passages, names, pack, block, group_rows):
    total, feats = queries.shape
    return pl.pallas_call(
        functools.partial(spread_kernel, group_rows),
        grid=(total // block,),
        in_specs=[
            pl.BlockSpec((block, feats), lambda i: (i, 0)),
            pl.BlockSpec((total, feats), lambda i: (0, 0)),
            pl.BlockSpec((block, LANES), lambda i: (i, 0)),
            pl.BlockSpec((block, LANES), lambda i: (i, 0)),
        ],
        out_specs=[
            pl.BlockSpec((block, feats), lambda i: (i, 0)),
            pl.BlockSpec((total, feats), lambda i: (0, 0)),
            pl.BlockSpec((1, total), lambda i: (0, 0)),
        ],
        out_shape=[
            jax.ShapeDtypeStruct((total, feats), jnp.float32),
            jax.ShapeDtypeStruct((total, feats), jnp.float32),
            jax.ShapeDtypeStruct((1, total), jnp.float32),
        ],
        compiler_params=pltpu.CompilerParams(vmem_limit_bytes=48 * 1024 * 1024),
    )(queries, passages, names, pack)


def per_device(activations, residual, down_weight, norm_gain, hard_owner, hard_row):
    everywhere = ("shard", "replica")
    n_shard, n_replica = lax.axis_size("shard"), lax.axis_size("replica")
    devices = n_shard * n_replica
    count = activations.shape[1]
    width = down_weight.shape[1]
    hidden = down_weight.shape[0]
    feats = width // devices
    total = count * devices
    block = 256 if total <= 2048 else 64

    name = jnp.pad(hard_owner * count + hard_row, ((0, 0), (0, LANES - HARD)))
    names = lax.all_gather(name, everywhere, axis=0, tiled=True)

    rows = activations.reshape(2 * count, activations.shape[2])
    spread_rows = lax.all_to_all(rows, "shard", split_axis=1, concat_axis=0, tiled=True)
    terms = jnp.dot(spread_rows, down_weight, preferred_element_type=jnp.float32)
    mixed = lax.psum_scatter(
        terms.astype(jnp.bfloat16), "shard", scatter_dimension=0, tiled=True
    ).astype(jnp.float32)
    all_rows = lax.all_gather(spread_rows, "replica", axis=0, tiled=False)
    all_rows = all_rows.reshape(n_replica, n_shard, 2, count, hidden)
    all_rows = all_rows.transpose(2, 1, 0, 3, 4).reshape(2 * total, hidden)

    stream = residual.reshape(2 * count, width).astype(jnp.float32) + mixed
    inv_rms, length, unit_f32 = normalize_rows(stream, norm_gain)
    unit = unit_f32.astype(jnp.bfloat16)
    held = unit.astype(jnp.float32)
    square = jnp.sum(held * held, axis=-1, keepdims=True)

    cut = unit.reshape(2 * count, n_replica, n_shard, feats).transpose(2, 1, 0, 3)
    cut = cut.reshape(devices, 2 * count, feats)
    cut = lax.all_to_all(cut, everywhere, split_axis=0, concat_axis=0, tiled=True)
    queries = cut[:, :count].reshape(total, feats)
    passages = cut[:, count:].reshape(total, feats)

    local_score = jnp.dot(unit[:count], unit[count:].T, preferred_element_type=jnp.float32)
    partial = pick_scores(queries, passages, names, block)[:, :HARD]
    partial = lax.all_to_all(
        partial.reshape(devices, count * HARD), everywhere, split_axis=0, concat_axis=0, tiled=True
    )
    hard_score = jnp.sum(partial, axis=0).reshape(count, HARD)
    losses, weights, shares = softmax_terms(local_score, hard_score)

    pack = jnp.concatenate(
        [
            weights,
            shares[:, count:],
            jnp.sum(shares, axis=1, keepdims=True),
            jnp.sum(shares[:, :count], axis=0)[:, None],
            inv_rms.reshape(2, count).T,
            length.reshape(2, count).T,
            square.reshape(2, count).T,
            losses,
        ],
        axis=1,
    )
    pack = jnp.pad(pack, ((0, 0), (0, LANES - pack.shape[1])))
    pack = lax.all_gather(pack, everywhere, axis=0, tiled=True)
    at = count + 2 * HARD

    def both(first):
        return jnp.stack([pack[:, first], pack[:, first + 1]])[:, :, None]

    grad_q, grad_p, extra = spread_grads(queries, passages, names, pack, block, count)
    dots = both(at) + jnp.stack([jnp.zeros((total,), jnp.float32), extra[0]])[:, :, None]
    inv_rms, length, square = both(at + 2), both(at + 4), both(at + 6)
    mean_loss = jnp.sum(pack[:, at + 8]) / total

    start = lax.axis_index("replica") * (width // n_replica) + lax.axis_index("shard") * feats
    gain = lax.dynamic_slice(norm_gain, (start,), (feats,))
    held = jnp.stack([queries, passages]).astype(jnp.float32)
    grad_unit = jnp.stack([grad_q, grad_p]) / sharpness_divisor
    grad_scaled = (grad_unit - held * dots) / length
    normed = held * length / gain
    gain_part = jnp.sum(grad_scaled * normed, axis=(0, 1))
    mean = (dots - dots * square) / width
    grad_stream = inv_rms * (grad_scaled * gain - normed * mean)
    grad_stream = grad_stream.astype(jnp.bfloat16).reshape(2 * total, feats)

    gain_grad = lax.all_gather(gain_part, everywhere, axis=0, tiled=True)
    gain_grad = gain_grad.reshape(n_shard, n_replica, feats).transpose(1, 0, 2).reshape(width)

    columns = lax.all_gather(grad_stream, "shard", axis=1, tiled=True)
    quarter = lax.dot_general(
        all_rows, columns, (((0,), (0,)), ((), ())), preferred_element_type=jnp.float32
    )
    weight_grad = lax.all_gather(
        quarter.astype(jnp.bfloat16), "replica", axis=1, tiled=True
    ).astype(jnp.float32)
    return (mean_loss, weight_grad, gain_grad)


def solution(mesh):
    in_specs = (
        P(None, ("shard", "replica"), None),
        P(None, ("shard", "replica"), None),
        P("shard", None),
        P(),
        P(("shard", "replica"), None),
        P(("shard", "replica"), None),
    )
    out_specs = (P(), P("shard", None), P())
    return jax.shard_map(
        per_device, mesh=mesh, in_specs=in_specs, out_specs=out_specs, check_vma=False
    )
```

```python
import functools

import jax
import jax.numpy as jnp
from jax import lax
from jax.experimental import pallas as pl
from jax.experimental.pallas import tpu as pltpu
from jax.sharding import PartitionSpec as P

HARD = 7
LANES = 128


epsilon = 1e-05
sharpness_divisor = 0.02


def normalize_rows(stream, norm_gain):
    inv_rms = lax.rsqrt(jnp.mean(stream * stream, axis=-1, keepdims=True) + epsilon)
    normed = stream * inv_rms
    scaled = normed * norm_gain
    length = jnp.sqrt(jnp.sum(scaled * scaled, axis=-1, keepdims=True))
    return (inv_rms, length, scaled / length)


def three_parts(values):
    parts = []
    for _ in range(3):
        part = lax.reduce_precision(values, 8, 7)
        parts.append(part.astype(jnp.bfloat16))
        values = values - part
    return parts


def softmax_terms(local_score, hard_score):
    width = local_score.shape[-1]
    logits = jnp.concatenate([local_score, hard_score], axis=-1) / sharpness_divisor
    expo = jnp.exp(logits)
    totals = jnp.sum(expo, axis=-1, keepdims=True)
    positive = jnp.diagonal(local_score) / sharpness_divisor
    losses = jnp.log(totals[:, 0]) - positive
    identity = jnp.eye(width, dtype=jnp.float32)
    target = jnp.concatenate([identity, jnp.zeros_like(hard_score)], axis=-1)
    weights = (expo / totals - target).astype(jnp.bfloat16).astype(jnp.float32)
    return (losses[:, None], weights, weights * logits)


def pick_kernel(q_ref, p_ref, name_ref, out_ref):
    score = lax.dot_general(
        q_ref[...], p_ref[...], (((1,), (1,)), ((), ())), preferred_element_type=jnp.float32
    )
    name = name_ref[...]
    lane, group = name % LANES, name // LANES
    found = jnp.zeros(out_ref.shape, jnp.float32)
    for block in range(p_ref.shape[0] // LANES):
        here = jnp.take_along_axis(score[:, block * LANES : (block + 1) * LANES], lane, axis=1)
        found = jnp.where(group == block, here, found)
    out_ref[...] = found


def pick_scores(queries, passages, names, block):
    total, feats = queries.shape
    return pl.pallas_call(
        pick_kernel,
        grid=(total // block,),
        in_specs=[
            pl.BlockSpec((block, feats), lambda i: (i, 0)),
            pl.BlockSpec((total, feats), lambda i: (0, 0)),
            pl.BlockSpec((block, LANES), lambda i: (i, 0)),
        ],
        out_specs=pl.BlockSpec((block, LANES), lambda i: (i, 0)),
        out_shape=jax.ShapeDtypeStruct((total, LANES), jnp.float32),
        compiler_params=pltpu.CompilerParams(vmem_limit_bytes=48 * 1024 * 1024),
    )(queries, passages, names)


def spread_kernel(group_rows, q_ref, p_ref, name_ref, pack_ref, gq_ref, gp_ref, tp_ref):
    step = pl.program_id(0)

    @pl.when(step == 0)
    def _():
        gp_ref[...] = jnp.zeros_like(gp_ref)
        tp_ref[...] = jnp.zeros_like(tp_ref)

    block, total = q_ref.shape[0], p_ref.shape[0]
    column = lax.broadcasted_iota(jnp.int32, (block, total), 1)
    weight = jnp.zeros((block, total), jnp.float32)
    share = jnp.zeros((block, total), jnp.float32)
    for k in range(HARD):
        hit = column == name_ref[:, k : k + 1]
        weight = jnp.where(hit, pack_ref[:, group_rows + k : group_rows + k + 1], weight)
        share = jnp.where(
            hit, pack_ref[:, group_rows + HARD + k : group_rows + HARD + k + 1], share
        )
    tp_ref[...] += jnp.sum(share, axis=0, keepdims=True)
    weight = weight.astype(jnp.bfloat16)
    gq_ref[...] = jnp.dot(weight, p_ref[...], preferred_element_type=jnp.float32)
    gp_ref[...] += lax.dot_general(
        weight, q_ref[...], (((0,), (0,)), ((), ())), preferred_element_type=jnp.float32
    )
    for part in range(block // group_rows):
        mine = slice(part * group_rows, (part + 1) * group_rows)
        there = pl.ds(pl.multiple_of(step * block + part * group_rows, group_rows), group_rows)
        local = pack_ref[mine, :group_rows].astype(jnp.bfloat16)
        gq_ref[mine, :] += jnp.dot(local, p_ref[there, :], preferred_element_type=jnp.float32)
        gp_ref[there, :] += lax.dot_general(
            local, q_ref[mine, :], (((0,), (0,)), ((), ())), preferred_element_type=jnp.float32
        )


def spread_grads(queries, passages, names, pack, block, group_rows):
    total, feats = queries.shape
    return pl.pallas_call(
        functools.partial(spread_kernel, group_rows),
        grid=(total // block,),
        in_specs=[
            pl.BlockSpec((block, feats), lambda i: (i, 0)),
            pl.BlockSpec((total, feats), lambda i: (0, 0)),
            pl.BlockSpec((block, LANES), lambda i: (i, 0)),
            pl.BlockSpec((block, LANES), lambda i: (i, 0)),
        ],
        out_specs=[
            pl.BlockSpec((block, feats), lambda i: (i, 0)),
            pl.BlockSpec((total, feats), lambda i: (0, 0)),
            pl.BlockSpec((1, total), lambda i: (0, 0)),
        ],
        out_shape=[
            jax.ShapeDtypeStruct((total, feats), jnp.float32),
            jax.ShapeDtypeStruct((total, feats), jnp.float32),
            jax.ShapeDtypeStruct((1, total), jnp.float32),
        ],
        compiler_params=pltpu.CompilerParams(vmem_limit_bytes=48 * 1024 * 1024),
    )(queries, passages, names, pack)


def per_device(activations, residual, down_weight, norm_gain, hard_owner, hard_row):
    everywhere = ("shard", "replica")
    n_shard, n_replica = lax.axis_size("shard"), lax.axis_size("replica")
    devices = n_shard * n_replica
    count = activations.shape[1]
    width = down_weight.shape[1]
    hidden = down_weight.shape[0]
    feats = width // devices
    total = count * devices
    block = 256 if total <= 2048 else 64

    rows = activations.reshape(2 * count, activations.shape[2])
    spread_rows = lax.all_to_all(rows, "shard", split_axis=1, concat_axis=0, tiled=True)
    terms = jnp.dot(spread_rows, down_weight, preferred_element_type=jnp.float32)
    mixed = lax.psum_scatter(
        terms.astype(jnp.bfloat16), "shard", scatter_dimension=0, tiled=True
    )
    all_rows = lax.all_gather(spread_rows, "replica", axis=0, tiled=False)
    mixed, all_rows = lax.optimization_barrier((mixed, all_rows))
    mixed = mixed.astype(jnp.float32)
    all_rows = all_rows.reshape(n_replica, n_shard, 2, count, hidden)
    all_rows = all_rows.transpose(2, 1, 0, 3, 4).reshape(2 * total, hidden)

    stream = residual.reshape(2 * count, width).astype(jnp.float32) + mixed
    inv_rms, length, unit_f32 = normalize_rows(stream, norm_gain)
    unit = unit_f32.astype(jnp.bfloat16)
    held = unit.astype(jnp.float32)
    square = jnp.sum(held * held, axis=-1, keepdims=True)

    cut = unit.reshape(2 * count, n_replica, n_shard, feats).transpose(2, 1, 0, 3)
    cut = cut.reshape(devices, 2 * count, feats)
    name = jnp.concatenate([hard_owner.T, hard_row.T]).astype(jnp.bfloat16).reshape(-1)
    taken = name.shape[0]
    extra_rows = -(-taken // (16 * feats)) * 16
    name = jnp.pad(name, (0, extra_rows * feats - taken)).reshape(1, extra_rows, feats)
    name = jnp.broadcast_to(name, (devices, extra_rows, feats))
    cut = jnp.concatenate([cut, name], axis=1)
    cut = lax.all_to_all(cut, everywhere, split_axis=0, concat_axis=0, tiled=True)
    queries = cut[:, :count].reshape(total, feats)
    passages = cut[:, count : 2 * count].reshape(total, feats)
    name = cut[:, 2 * count :].reshape(devices, -1)[:, :taken].astype(jnp.int32)
    name = name.reshape(devices, 2, HARD, count)
    names = (name[:, 0] * count + name[:, 1]).transpose(0, 2, 1).reshape(total, HARD)
    names = jnp.pad(names, ((0, 0), (0, LANES - HARD)))

    local_score = jnp.dot(unit[:count], unit[count:].T, preferred_element_type=jnp.float32)
    partial = pick_scores(queries, passages, names, block)[:, :HARD]
    partial = lax.all_to_all(
        partial.reshape(devices, count * HARD), everywhere, split_axis=0, concat_axis=0, tiled=True
    )
    hard_score = jnp.sum(partial, axis=0).reshape(count, HARD)
    losses, weights, shares = softmax_terms(local_score, hard_score)

    scalars = jnp.concatenate(
        [
            shares[:, count:],
            jnp.sum(shares, axis=1, keepdims=True),
            jnp.sum(shares[:, :count], axis=0)[:, None],
            inv_rms.reshape(2, count).T,
            length.reshape(2, count).T,
            square.reshape(2, count).T,
            losses,
        ],
        axis=1,
    )
    pack = jnp.concatenate([weights.astype(jnp.bfloat16), *three_parts(scalars)], axis=1)
    pack = jnp.pad(pack, ((0, 0), (0, LANES - pack.shape[1])))
    pack = jnp.broadcast_to(pack, (devices, count, LANES))
    pack = lax.all_to_all(pack, everywhere, split_axis=0, concat_axis=0, tiled=True)
    pack = pack.reshape(total, LANES).astype(jnp.float32)
    first, some = count + HARD, scalars.shape[1]
    scalars = sum(pack[:, first + part * some : first + (part + 1) * some] for part in range(3))
    pack = jnp.concatenate([pack[:, :first], scalars], axis=1)
    pack = jnp.pad(pack, ((0, 0), (0, LANES - pack.shape[1])))
    at = count + 2 * HARD

    def both(first):
        return jnp.stack([pack[:, first], pack[:, first + 1]])[:, :, None]

    grad_q, grad_p, extra = spread_grads(queries, passages, names, pack, block, count)
    dots = both(at) + jnp.stack([jnp.zeros((total,), jnp.float32), extra[0]])[:, :, None]
    inv_rms, length, square = both(at + 2), both(at + 4), both(at + 6)
    mean_loss = jnp.sum(pack[:, at + 8]) / total

    start = lax.axis_index("replica") * (width // n_replica) + lax.axis_index("shard") * feats
    gain = lax.dynamic_slice(norm_gain, (start,), (feats,))
    held = jnp.stack([queries, passages]).astype(jnp.float32)
    grad_unit = jnp.stack([grad_q, grad_p]) / sharpness_divisor
    grad_scaled = (grad_unit - held * dots) / length
    normed = held * length / gain
    gain_part = jnp.sum(grad_scaled * normed, axis=(0, 1))
    mean = (dots - dots * square) / width
    grad_stream = inv_rms * (grad_scaled * gain - normed * mean)
    grad_stream = grad_stream.astype(jnp.bfloat16).reshape(2 * total, feats)

    extra = jnp.pad(jnp.stack(three_parts(gain_part)), ((0, 13), (0, 0)))
    columns = lax.all_gather(
        jnp.concatenate([grad_stream, extra], axis=0), "shard", axis=1, tiled=True
    )
    quarter = lax.dot_general(
        all_rows, columns[: 2 * total], (((0,), (0,)), ((), ())), preferred_element_type=jnp.float32
    )
    quarter = jnp.concatenate([quarter.astype(jnp.bfloat16), columns[2 * total :]], axis=0)
    gathered = lax.all_gather(quarter, "replica", axis=1, tiled=True).astype(jnp.float32)
    weight_grad = gathered[:hidden]
    gain_grad = jnp.sum(gathered[hidden : hidden + 3], axis=0)
    return (mean_loss, weight_grad, gain_grad)


def solution(mesh):
    in_specs = (
        P(None, ("shard", "replica"), None),
        P(None, ("shard", "replica"), None),
        P("shard", None),
        P(),
        P(("shard", "replica"), None),
        P(("shard", "replica"), None),
    )
    out_specs = (P(), P("shard", None), P())
    return jax.shard_map(
        per_device, mesh=mesh, in_specs=in_specs, out_specs=out_specs, check_vma=False
    )
```

```python
import functools

import jax
import jax.numpy as jnp
from jax import lax
from jax.experimental import pallas as pl
from jax.experimental.pallas import tpu as pltpu
from jax.sharding import PartitionSpec as P

HARD = 7
LANES = 128
PIECES = 2


epsilon = 1e-05
sharpness_divisor = 0.02


def normalize_rows(stream, norm_gain):
    inv_rms = lax.rsqrt(jnp.mean(stream * stream, axis=-1, keepdims=True) + epsilon)
    normed = stream * inv_rms
    scaled = normed * norm_gain
    length = jnp.sqrt(jnp.sum(scaled * scaled, axis=-1, keepdims=True))
    return (inv_rms, length, scaled / length)


def three_parts(values):
    parts = []
    for _ in range(3):
        part = lax.reduce_precision(values, 8, 7)
        parts.append(part.astype(jnp.bfloat16))
        values = values - part
    return parts


def softmax_terms(local_score, hard_score):
    width = local_score.shape[-1]
    logits = jnp.concatenate([local_score, hard_score], axis=-1) / sharpness_divisor
    expo = jnp.exp(logits)
    totals = jnp.sum(expo, axis=-1, keepdims=True)
    positive = jnp.diagonal(local_score) / sharpness_divisor
    losses = jnp.log(totals[:, 0]) - positive
    identity = jnp.eye(width, dtype=jnp.float32)
    target = jnp.concatenate([identity, jnp.zeros_like(hard_score)], axis=-1)
    weights = (expo / totals - target).astype(jnp.bfloat16).astype(jnp.float32)
    return (losses[:, None], weights, weights * logits)


def pick_kernel(q_ref, p_ref, name_ref, out_ref):
    score = lax.dot_general(
        q_ref[...], p_ref[...], (((1,), (1,)), ((), ())), preferred_element_type=jnp.float32
    )
    name = name_ref[...]
    lane, group = name % LANES, name // LANES
    found = jnp.zeros(out_ref.shape, jnp.float32)
    for block in range(p_ref.shape[0] // LANES):
        here = jnp.take_along_axis(score[:, block * LANES : (block + 1) * LANES], lane, axis=1)
        found = jnp.where(group == block, here, found)
    out_ref[...] = found


def pick_scores(queries, passages, names, block):
    total, feats = queries.shape
    return pl.pallas_call(
        pick_kernel,
        grid=(total // block,),
        in_specs=[
            pl.BlockSpec((block, feats), lambda i: (i, 0)),
            pl.BlockSpec((total, feats), lambda i: (0, 0)),
            pl.BlockSpec((block, LANES), lambda i: (i, 0)),
        ],
        out_specs=pl.BlockSpec((block, LANES), lambda i: (i, 0)),
        out_shape=jax.ShapeDtypeStruct((total, LANES), jnp.float32),
        compiler_params=pltpu.CompilerParams(vmem_limit_bytes=48 * 1024 * 1024),
    )(queries, passages, names)


def spread_kernel(
    group_rows, q_ref, p_ref, name_ref, pack_ref, widen_ref, gq_ref, gp_ref, tp_ref
):
    step = pl.program_id(0)

    @pl.when(step == 0)
    def _():
        gp_ref[...] = jnp.zeros_like(gp_ref)
        tp_ref[...] = jnp.zeros_like(tp_ref)

    block, total = q_ref.shape[0], p_ref.shape[0]
    name = name_ref[...]
    owner, row = name // group_rows, (name % group_rows).astype(jnp.float32)
    lane = lax.broadcasted_iota(jnp.int32, (block, LANES), 1)
    rows = jnp.full((block, LANES), -1.0, jnp.float32)
    weight = jnp.zeros((block, LANES), jnp.float32)
    share = jnp.zeros((block, LANES), jnp.float32)
    for k in range(HARD):
        hit = lane == owner[:, k : k + 1]
        at = group_rows + k
        rows = jnp.where(hit, row[:, k : k + 1], rows)
        weight = jnp.where(hit, pack_ref[:, at : at + 1], weight)
        share = jnp.where(hit, pack_ref[:, at + HARD : at + HARD + 1], share)

    def widen(values):
        return jnp.dot(
            values.astype(jnp.bfloat16), widen_ref[...], preferred_element_type=jnp.float32
        )

    column = lax.broadcasted_iota(jnp.int32, (1, total), 1) % group_rows
    hit = widen(rows) == column.astype(jnp.float32)
    tp_ref[...] += jnp.sum(jnp.where(hit, widen(share), 0.0), axis=0, keepdims=True)
    weight = jnp.where(hit, widen(weight), 0.0).astype(jnp.bfloat16)
    gq_ref[...] = jnp.dot(weight, p_ref[...], preferred_element_type=jnp.float32)
    gp_ref[...] += lax.dot_general(
        weight, q_ref[...], (((0,), (0,)), ((), ())), preferred_element_type=jnp.float32
    )
    for part in range(block // group_rows):
        mine = slice(part * group_rows, (part + 1) * group_rows)
        there = pl.ds(pl.multiple_of(step * block + part * group_rows, group_rows), group_rows)
        local = pack_ref[mine, :group_rows].astype(jnp.bfloat16)
        gq_ref[mine, :] += jnp.dot(local, p_ref[there, :], preferred_element_type=jnp.float32)
        gp_ref[there, :] += lax.dot_general(
            local, q_ref[mine, :], (((0,), (0,)), ((), ())), preferred_element_type=jnp.float32
        )


def spread_grads(queries, passages, names, pack, block, group_rows):
    total, feats = queries.shape
    owner = jnp.arange(total, dtype=jnp.int32)[None, :] // group_rows
    widen = (jnp.arange(LANES, dtype=jnp.int32)[:, None] == owner).astype(jnp.bfloat16)
    return pl.pallas_call(
        functools.partial(spread_kernel, group_rows),
        grid=(total // block,),
        in_specs=[
            pl.BlockSpec((block, feats), lambda i: (i, 0)),
            pl.BlockSpec((total, feats), lambda i: (0, 0)),
            pl.BlockSpec((block, LANES), lambda i: (i, 0)),
            pl.BlockSpec((block, LANES), lambda i: (i, 0)),
            pl.BlockSpec((LANES, total), lambda i: (0, 0)),
        ],
        out_specs=[
            pl.BlockSpec((block, feats), lambda i: (i, 0)),
            pl.BlockSpec((total, feats), lambda i: (0, 0)),
            pl.BlockSpec((1, total), lambda i: (0, 0)),
        ],
        out_shape=[
            jax.ShapeDtypeStruct((total, feats), jnp.float32),
            jax.ShapeDtypeStruct((total, feats), jnp.float32),
            jax.ShapeDtypeStruct((1, total), jnp.float32),
        ],
        compiler_params=pltpu.CompilerParams(vmem_limit_bytes=48 * 1024 * 1024),
    )(queries, passages, names, pack, widen)


def lay_kernel(*refs):
    *pieces, out_ref = refs
    span = pieces[0].shape[2]
    for at, piece in enumerate(pieces):
        out_ref[:, at * span : (at + 1) * span] = piece[0].astype(jnp.float32)


def lay_columns(pieces, hidden):
    parts, _, span = pieces[0].shape
    block = min(hidden, 256)
    wide = span * len(pieces)
    return pl.pallas_call(
        lay_kernel,
        grid=(parts, hidden // block),
        in_specs=[pl.BlockSpec((1, block, span), lambda r, i: (r, i, 0)) for _ in pieces],
        out_specs=pl.BlockSpec((block, wide), lambda r, i: (i, r)),
        out_shape=jax.ShapeDtypeStruct((hidden, parts * wide), jnp.float32),
        compiler_params=pltpu.CompilerParams(vmem_limit_bytes=32 * 1024 * 1024),
    )(*pieces)


def per_device(activations, residual, down_weight, norm_gain, hard_owner, hard_row):
    everywhere = ("shard", "replica")
    n_shard, n_replica = lax.axis_size("shard"), lax.axis_size("replica")
    devices = n_shard * n_replica
    count = activations.shape[1]
    width = down_weight.shape[1]
    hidden = down_weight.shape[0]
    feats = width // devices
    total = count * devices
    block = 256 if total <= 2048 else 64

    rows = activations.reshape(2 * count, activations.shape[2])
    spread_rows = lax.all_to_all(rows, "shard", split_axis=1, concat_axis=0, tiled=True)
    terms = jnp.dot(spread_rows, down_weight, preferred_element_type=jnp.float32)
    mixed = lax.psum_scatter(
        terms.astype(jnp.bfloat16), "shard", scatter_dimension=0, tiled=True
    )
    all_rows = lax.all_gather(spread_rows, "replica", axis=0, tiled=False)
    mixed, all_rows = lax.optimization_barrier((mixed, all_rows))
    mixed = mixed.astype(jnp.float32)
    all_rows = all_rows.reshape(n_replica, n_shard, 2, count, hidden)
    all_rows = all_rows.transpose(2, 1, 0, 3, 4).reshape(2 * total, hidden)

    stream = residual.reshape(2 * count, width).astype(jnp.float32) + mixed
    inv_rms, length, unit_f32 = normalize_rows(stream, norm_gain)
    unit = unit_f32.astype(jnp.bfloat16)
    held = unit.astype(jnp.float32)
    square = jnp.sum(held * held, axis=-1, keepdims=True)

    small = feats // PIECES
    cut = unit.reshape(2 * count, n_replica, PIECES, n_shard, small).transpose(3, 1, 0, 2, 4)
    cut = cut.reshape(devices, 2 * count, feats)
    name = jnp.concatenate([hard_owner.T, hard_row.T]).astype(jnp.bfloat16).reshape(-1)
    taken = name.shape[0]
    extra_rows = -(-taken // (16 * feats)) * 16
    name = jnp.pad(name, (0, extra_rows * feats - taken)).reshape(1, extra_rows, feats)
    name = jnp.broadcast_to(name, (devices, extra_rows, feats))
    cut = jnp.concatenate([cut, name], axis=1)
    cut = lax.all_to_all(cut, everywhere, split_axis=0, concat_axis=0, tiled=True)
    queries = cut[:, :count].reshape(total, feats)
    passages = cut[:, count : 2 * count].reshape(total, feats)
    name = cut[:, 2 * count :].reshape(devices, -1)[:, :taken].astype(jnp.int32)
    name = name.reshape(devices, 2, HARD, count)
    names = (name[:, 0] * count + name[:, 1]).transpose(0, 2, 1).reshape(total, HARD)
    names = jnp.pad(names, ((0, 0), (0, LANES - HARD)))

    local_score = jnp.dot(unit[:count], unit[count:].T, preferred_element_type=jnp.float32)
    partial = pick_scores(queries, passages, names, block)[:, :HARD]
    partial = lax.all_to_all(
        partial.reshape(devices, count * HARD), everywhere, split_axis=0, concat_axis=0, tiled=True
    )
    hard_score = jnp.sum(partial, axis=0).reshape(count, HARD)
    losses, weights, shares = softmax_terms(local_score, hard_score)

    scalars = jnp.concatenate(
        [
            shares[:, count:],
            jnp.sum(shares, axis=1, keepdims=True),
            jnp.sum(shares[:, :count], axis=0)[:, None],
            inv_rms.reshape(2, count).T,
            length.reshape(2, count).T,
            square.reshape(2, count).T,
            losses,
        ],
        axis=1,
    )
    pack = jnp.concatenate([weights.astype(jnp.bfloat16), *three_parts(scalars)], axis=1)
    pack = jnp.pad(pack, ((0, 0), (0, LANES - pack.shape[1])))
    pack = jnp.broadcast_to(pack, (devices, count, LANES))
    pack = lax.all_to_all(pack, everywhere, split_axis=0, concat_axis=0, tiled=True)
    pack = pack.reshape(total, LANES).astype(jnp.float32)
    first, some = count + HARD, scalars.shape[1]
    scalars = sum(pack[:, first + part * some : first + (part + 1) * some] for part in range(3))
    pack = jnp.concatenate([pack[:, :first], scalars], axis=1)
    pack = jnp.pad(pack, ((0, 0), (0, LANES - pack.shape[1])))
    at = count + 2 * HARD

    def both(first):
        return jnp.stack([pack[:, first], pack[:, first + 1]])[:, :, None]

    grad_q, grad_p, extra = spread_grads(queries, passages, names, pack, block, count)
    dots = both(at) + jnp.stack([jnp.zeros((total,), jnp.float32), extra[0]])[:, :, None]
    inv_rms, length, square = both(at + 2), both(at + 4), both(at + 6)
    mean_loss = jnp.sum(pack[:, at + 8]) / total

    gain = norm_gain.reshape(n_replica, PIECES, n_shard, small)
    gain = lax.dynamic_index_in_dim(gain, lax.axis_index("replica"), 0, keepdims=False)
    gain = lax.dynamic_index_in_dim(gain, lax.axis_index("shard"), 1, keepdims=False)
    gain = gain.reshape(feats)
    held = jnp.stack([queries, passages]).astype(jnp.float32)
    grad_unit = jnp.stack([grad_q, grad_p]) / sharpness_divisor
    grad_scaled = (grad_unit - held * dots) / length
    normed = held * length / gain
    gain_part = jnp.sum(grad_scaled * normed, axis=(0, 1))
    mean = (dots - dots * square) / width
    grad_stream = inv_rms * (grad_scaled * gain - normed * mean)
    grad_stream = grad_stream.astype(jnp.bfloat16).reshape(2 * total, feats)

    extra = jnp.pad(jnp.stack(three_parts(gain_part)), ((0, 13), (0, 0)))
    sent = jnp.concatenate([grad_stream, extra], axis=0).T
    pieces = []
    for piece in range(PIECES):
        mine = sent[piece * small : (piece + 1) * small]
        columns = lax.all_gather(mine, "shard", axis=0, tiled=True)
        product = lax.dot_general(
            all_rows,
            columns[:, : 2 * total],
            (((0,), (1,)), ((), ())),
            preferred_element_type=jnp.float32,
        ).astype(jnp.bfloat16)
        product = jnp.concatenate([product, columns[:, 2 * total :].T], axis=0)
        pieces.append(lax.all_gather(product, "replica", axis=0, tiled=False))
    weight_grad = lay_columns(pieces, hidden)
    gain_grad = jnp.stack([piece[:, hidden : hidden + 3] for piece in pieces], axis=1)
    gain_grad = jnp.sum(gain_grad.astype(jnp.float32), axis=2).reshape(width)
    return (mean_loss, weight_grad, gain_grad)


def solution(mesh):
    in_specs = (
        P(None, ("shard", "replica"), None),
        P(None, ("shard", "replica"), None),
        P("shard", None),
        P(),
        P(("shard", "replica"), None),
        P(("shard", "replica"), None),
    )
    out_specs = (P(), P("shard", None), P())
    return jax.shard_map(
        per_device, mesh=mesh, in_specs=in_specs, out_specs=out_specs, check_vma=False
    )
```

```python
import functools

import jax
import jax.numpy as jnp
from jax import lax
from jax.experimental import pallas as pl
from jax.experimental.pallas import tpu as pltpu
from jax.sharding import PartitionSpec as P

HARD = 7
LANES = 128
PIECES = 2


epsilon = 1e-05
sharpness_divisor = 0.02


def normalize_rows(stream, norm_gain):
    inv_rms = lax.rsqrt(jnp.mean(stream * stream, axis=-1, keepdims=True) + epsilon)
    normed = stream * inv_rms
    scaled = normed * norm_gain
    length = jnp.sqrt(jnp.sum(scaled * scaled, axis=-1, keepdims=True))
    return (inv_rms, length, scaled / length)


def three_parts(values):
    parts = []
    for _ in range(3):
        part = lax.reduce_precision(values, 8, 7)
        parts.append(part.astype(jnp.bfloat16))
        values = values - part
    return parts


def softmax_terms(local_score, hard_score):
    width = local_score.shape[-1]
    logits = jnp.concatenate([local_score, hard_score], axis=-1) / sharpness_divisor
    expo = jnp.exp(logits)
    totals = jnp.sum(expo, axis=-1, keepdims=True)
    positive = jnp.diagonal(local_score) / sharpness_divisor
    losses = jnp.log(totals[:, 0]) - positive
    identity = jnp.eye(width, dtype=jnp.float32)
    target = jnp.concatenate([identity, jnp.zeros_like(hard_score)], axis=-1)
    weights = (expo / totals - target).astype(jnp.bfloat16).astype(jnp.float32)
    return (losses[:, None], weights, weights * logits)


def pick_kernel(q_ref, p_ref, name_ref, out_ref):
    score = lax.dot_general(
        q_ref[...], p_ref[...], (((1,), (1,)), ((), ())), preferred_element_type=jnp.float32
    )
    name = name_ref[...]
    lane, group = name % LANES, name // LANES
    found = jnp.zeros(out_ref.shape, jnp.float32)
    for block in range(p_ref.shape[0] // LANES):
        here = jnp.take_along_axis(score[:, block * LANES : (block + 1) * LANES], lane, axis=1)
        found = jnp.where(group == block, here, found)
    out_ref[...] = found


def pick_scores(queries, passages, names, block):
    total, feats = queries.shape
    return pl.pallas_call(
        pick_kernel,
        grid=(total // block,),
        in_specs=[
            pl.BlockSpec((block, feats), lambda i: (i, 0)),
            pl.BlockSpec((total, feats), lambda i: (0, 0)),
            pl.BlockSpec((block, LANES), lambda i: (i, 0)),
        ],
        out_specs=pl.BlockSpec((block, LANES), lambda i: (i, 0)),
        out_shape=jax.ShapeDtypeStruct((total, LANES), jnp.float32),
        compiler_params=pltpu.CompilerParams(vmem_limit_bytes=48 * 1024 * 1024),
    )(queries, passages, names)


def spread_kernel(
    group_rows, q_ref, p_ref, name_ref, pack_ref, widen_ref, gq_ref, gp_ref, tp_ref
):
    step = pl.program_id(0)

    @pl.when(step == 0)
    def _():
        gp_ref[...] = jnp.zeros_like(gp_ref)
        tp_ref[...] = jnp.zeros_like(tp_ref)

    block, total = q_ref.shape[0], p_ref.shape[0]
    name = name_ref[...]
    owner, row = name // group_rows, (name % group_rows).astype(jnp.float32)
    lane = lax.broadcasted_iota(jnp.int32, (block, LANES), 1)
    rows = jnp.full((block, LANES), -1.0, jnp.float32)
    weight = jnp.zeros((block, LANES), jnp.float32)
    share = jnp.zeros((block, LANES), jnp.float32)
    for k in range(HARD):
        hit = lane == owner[:, k : k + 1]
        at = group_rows + k
        rows = jnp.where(hit, row[:, k : k + 1], rows)
        weight = jnp.where(hit, pack_ref[:, at : at + 1], weight)
        share = jnp.where(hit, pack_ref[:, at + HARD : at + HARD + 1], share)

    def widen(values):
        return jnp.dot(
            values.astype(jnp.bfloat16), widen_ref[...], preferred_element_type=jnp.float32
        )

    column = lax.broadcasted_iota(jnp.int32, (1, total), 1) % group_rows
    hit = widen(rows) == column.astype(jnp.float32)
    tp_ref[...] += jnp.sum(jnp.where(hit, widen(share), 0.0), axis=0, keepdims=True)
    weight = jnp.where(hit, widen(weight), 0.0).astype(jnp.bfloat16)
    gq_ref[...] = jnp.dot(weight, p_ref[...], preferred_element_type=jnp.float32)
    gp_ref[...] += lax.dot_general(
        weight, q_ref[...], (((0,), (0,)), ((), ())), preferred_element_type=jnp.float32
    )
    for part in range(block // group_rows):
        mine = slice(part * group_rows, (part + 1) * group_rows)
        there = pl.ds(pl.multiple_of(step * block + part * group_rows, group_rows), group_rows)
        local = pack_ref[mine, :group_rows].astype(jnp.bfloat16)
        gq_ref[mine, :] += jnp.dot(local, p_ref[there, :], preferred_element_type=jnp.float32)
        gp_ref[there, :] += lax.dot_general(
            local, q_ref[mine, :], (((0,), (0,)), ((), ())), preferred_element_type=jnp.float32
        )


def spread_grads(queries, passages, names, pack, block, group_rows):
    total, feats = queries.shape
    owner = jnp.arange(total, dtype=jnp.int32)[None, :] // group_rows
    widen = (jnp.arange(LANES, dtype=jnp.int32)[:, None] == owner).astype(jnp.bfloat16)
    return pl.pallas_call(
        functools.partial(spread_kernel, group_rows),
        grid=(total // block,),
        in_specs=[
            pl.BlockSpec((block, feats), lambda i: (i, 0)),
            pl.BlockSpec((total, feats), lambda i: (0, 0)),
            pl.BlockSpec((block, LANES), lambda i: (i, 0)),
            pl.BlockSpec((block, LANES), lambda i: (i, 0)),
            pl.BlockSpec((LANES, total), lambda i: (0, 0)),
        ],
        out_specs=[
            pl.BlockSpec((block, feats), lambda i: (i, 0)),
            pl.BlockSpec((total, feats), lambda i: (0, 0)),
            pl.BlockSpec((1, total), lambda i: (0, 0)),
        ],
        out_shape=[
            jax.ShapeDtypeStruct((total, feats), jnp.float32),
            jax.ShapeDtypeStruct((total, feats), jnp.float32),
            jax.ShapeDtypeStruct((1, total), jnp.float32),
        ],
        compiler_params=pltpu.CompilerParams(vmem_limit_bytes=48 * 1024 * 1024),
    )(queries, passages, names, pack, widen)


def lay_kernel(count, me_ref, *refs):
    *pieces, out_ref = refs
    span = pieces[0].shape[1]
    wide = span * PIECES
    for piece in range(PIECES):
        for turn in range(count):
            at = (me_ref[0] ^ turn) * wide + piece * span
            here = pieces[piece * count + turn][...].astype(jnp.float32)
            out_ref[:, pl.ds(pl.multiple_of(at, span), span)] = here


def lay_columns(me, pieces, hidden):
    count, span = len(pieces[0]), pieces[0][0].shape[1]
    block = min(hidden, 128)
    width = count * PIECES * span
    return pl.pallas_call(
        functools.partial(lay_kernel, count),
        grid_spec=pltpu.PrefetchScalarGridSpec(
            num_scalar_prefetch=1,
            grid=(hidden // block,),
            in_specs=[pl.BlockSpec((block, span), lambda i, m: (i, 0))] * (PIECES * count),
            out_specs=pl.BlockSpec((block, width), lambda i, m: (i, 0)),
        ),
        out_shape=jax.ShapeDtypeStruct((hidden, width), jnp.float32),
        compiler_params=pltpu.CompilerParams(vmem_limit_bytes=32 * 1024 * 1024),
    )(me.reshape(1), *[block for piece in pieces for block in piece])


def exchange(mine):
    count = lax.axis_size("replica")

    def swap(block, turn):
        return lax.ppermute(block, "replica", [(i, i ^ turn) for i in range(count)])

    if count != 4:
        return [mine] + [swap(mine, turn) for turn in range(1, count)]
    first, second = swap(mine, 1), swap(mine, 2)
    half = mine.shape[0] // 32 * 16
    across = [swap(first[:half], 2), swap(second[half:], 1)]
    return [mine, first, second, jnp.concatenate(across, axis=0)]


def per_device(activations, residual, down_weight, norm_gain, hard_owner, hard_row):
    everywhere = ("shard", "replica")
    n_shard, n_replica = lax.axis_size("shard"), lax.axis_size("replica")
    devices = n_shard * n_replica
    count = activations.shape[1]
    width = down_weight.shape[1]
    hidden = down_weight.shape[0]
    feats = width // devices
    total = count * devices
    block = 256 if total <= 2048 else 64

    rows = activations.reshape(2 * count, activations.shape[2])
    spread_rows = lax.all_to_all(rows, "shard", split_axis=1, concat_axis=0, tiled=True)
    terms = jnp.dot(spread_rows, down_weight, preferred_element_type=jnp.float32)
    mixed = lax.psum_scatter(
        terms.astype(jnp.bfloat16), "shard", scatter_dimension=0, tiled=True
    )
    all_rows = lax.all_gather(spread_rows, "replica", axis=0, tiled=False)
    mixed, all_rows = lax.optimization_barrier((mixed, all_rows))
    mixed = mixed.astype(jnp.float32)
    all_rows = all_rows.reshape(n_replica, n_shard, 2, count, hidden)
    all_rows = all_rows.transpose(2, 1, 0, 3, 4).reshape(2 * total, hidden)

    stream = residual.reshape(2 * count, width).astype(jnp.float32) + mixed
    inv_rms, length, unit_f32 = normalize_rows(stream, norm_gain)
    unit = unit_f32.astype(jnp.bfloat16)
    held = unit.astype(jnp.float32)
    square = jnp.sum(held * held, axis=-1, keepdims=True)

    small = feats // PIECES
    cut = unit.reshape(2 * count, n_replica, PIECES, n_shard, small).transpose(3, 1, 0, 2, 4)
    cut = cut.reshape(devices, 2 * count, feats)
    name = jnp.concatenate([hard_owner.T, hard_row.T]).astype(jnp.bfloat16).reshape(-1)
    taken = name.shape[0]
    extra_rows = -(-taken // (16 * feats)) * 16
    name = jnp.pad(name, (0, extra_rows * feats - taken)).reshape(1, extra_rows, feats)
    name = jnp.broadcast_to(name, (devices, extra_rows, feats))
    cut = jnp.concatenate([cut, name], axis=1)
    cut = lax.all_to_all(cut, everywhere, split_axis=0, concat_axis=0, tiled=True)
    queries = cut[:, :count].reshape(total, feats)
    passages = cut[:, count : 2 * count].reshape(total, feats)
    name = cut[:, 2 * count :].reshape(devices, -1)[:, :taken].astype(jnp.int32)
    name = name.reshape(devices, 2, HARD, count)
    names = (name[:, 0] * count + name[:, 1]).transpose(0, 2, 1).reshape(total, HARD)
    names = jnp.pad(names, ((0, 0), (0, LANES - HARD)))

    local_score = jnp.dot(unit[:count], unit[count:].T, preferred_element_type=jnp.float32)
    partial = pick_scores(queries, passages, names, block)[:, :HARD]
    partial = lax.all_to_all(
        partial.reshape(devices, count * HARD), everywhere, split_axis=0, concat_axis=0, tiled=True
    )
    hard_score = jnp.sum(partial, axis=0).reshape(count, HARD)
    losses, weights, shares = softmax_terms(local_score, hard_score)

    scalars = jnp.concatenate(
        [
            shares[:, count:],
            jnp.sum(shares, axis=1, keepdims=True),
            jnp.sum(shares[:, :count], axis=0)[:, None],
            inv_rms.reshape(2, count).T,
            length.reshape(2, count).T,
            square.reshape(2, count).T,
            losses,
        ],
        axis=1,
    )
    pack = jnp.concatenate([weights.astype(jnp.bfloat16), *three_parts(scalars)], axis=1)
    pack = jnp.pad(pack, ((0, 0), (0, LANES - pack.shape[1])))
    pack = jnp.broadcast_to(pack, (devices, count, LANES))
    pack = lax.all_to_all(pack, everywhere, split_axis=0, concat_axis=0, tiled=True)
    pack = pack.reshape(total, LANES).astype(jnp.float32)
    first, some = count + HARD, scalars.shape[1]
    scalars = sum(pack[:, first + part * some : first + (part + 1) * some] for part in range(3))
    pack = jnp.concatenate([pack[:, :first], scalars], axis=1)
    pack = jnp.pad(pack, ((0, 0), (0, LANES - pack.shape[1])))
    at = count + 2 * HARD

    def both(first):
        return jnp.stack([pack[:, first], pack[:, first + 1]])[:, :, None]

    grad_q, grad_p, extra = spread_grads(queries, passages, names, pack, block, count)
    dots = both(at) + jnp.stack([jnp.zeros((total,), jnp.float32), extra[0]])[:, :, None]
    inv_rms, length, square = both(at + 2), both(at + 4), both(at + 6)
    mean_loss = jnp.sum(pack[:, at + 8]) / total

    gain = norm_gain.reshape(n_replica, PIECES, n_shard, small)
    gain = lax.dynamic_index_in_dim(gain, lax.axis_index("replica"), 0, keepdims=False)
    gain = lax.dynamic_index_in_dim(gain, lax.axis_index("shard"), 1, keepdims=False)
    gain = gain.reshape(feats)
    held = jnp.stack([queries, passages]).astype(jnp.float32)
    grad_unit = jnp.stack([grad_q, grad_p]) / sharpness_divisor
    grad_scaled = (grad_unit - held * dots) / length
    normed = held * length / gain
    gain_part = jnp.sum(grad_scaled * normed, axis=(0, 1))
    mean = (dots - dots * square) / width
    grad_stream = inv_rms * (grad_scaled * gain - normed * mean)
    grad_stream = grad_stream.astype(jnp.bfloat16).reshape(2 * total, feats)

    extra = jnp.pad(jnp.stack(three_parts(gain_part)), ((0, 13), (0, 0)))
    sent = jnp.concatenate([grad_stream, extra], axis=0).T
    pieces = []
    for piece in range(PIECES):
        mine = sent[piece * small : (piece + 1) * small]
        columns = lax.all_gather(mine, "shard", axis=0, tiled=True)
        product = lax.dot_general(
            all_rows,
            columns[:, : 2 * total],
            (((0,), (1,)), ((), ())),
            preferred_element_type=jnp.float32,
        ).astype(jnp.bfloat16)
        product = jnp.concatenate([product, columns[:, 2 * total :].T], axis=0)
        pieces.append(exchange(product))
    me = lax.axis_index("replica")
    weight_grad = lay_columns(me, pieces, hidden)
    gain_grad = jnp.stack(
        [
            jnp.stack([jnp.sum(b[hidden : hidden + 3].astype(jnp.float32), axis=0) for b in blocks])
            for blocks in pieces
        ],
        axis=1,
    )
    gain_grad = gain_grad[jnp.arange(n_replica) ^ me].reshape(width)
    return (mean_loss, weight_grad, gain_grad)


def solution(mesh):
    in_specs = (
        P(None, ("shard", "replica"), None),
        P(None, ("shard", "replica"), None),
        P("shard", None),
        P(),
        P(("shard", "replica"), None),
        P(("shard", "replica"), None),
    )
    out_specs = (P(), P("shard", None), P())
    return jax.shard_map(
        per_device, mesh=mesh, in_specs=in_specs, out_specs=out_specs, check_vma=False
    )
```
